32 devices in a mesh: row: 4 (over z), col: 4 (over y, x), dp: 2 (over core).
Axes of the slice: x: 2, y: 2, z: 4, core: 2. Of those that a mesh axis runs over, the one named last changes fastest.
Arguments:
- tokens: bfloat16 [1024, 4096], P(('col', 'dp'), 'row'), may hold values from -6 to 6
- timesteps: int32 [4], replicated, may hold values from 0 to 999
- ada_weight: bfloat16 [3, 4096, 4096], P(None, 'col', 'row'), may hold values from -0.09375 to 0.09375
- up_weight: bfloat16 [4096, 16384], P('row', 'col'), may hold values from -0.90625 to 0.90625
- down_weight: bfloat16 [16384, 4096], P('col', 'row'), may hold values from -0.046875 to 0.046875
- cotangent: bfloat16 [1024, 4096], P(('col', 'dp'), 'row'), may hold values from -6 to 6
Outputs:
- grad_tokens: bfloat16 [1024, 4096], P(('col', 'dp'), 'row')
- grad_ada: float32 [3, 4096, 4096], P(None, 'col', 'row')
- grad_up: float32 [4096, 16384], P('row', ('col', 'dp'))
- grad_down: float32 [16384, 4096], P(('col', 'dp'), 'row')
The draws below stay inside these ranges and needn't reach their ends.
All inputs are finite; a program needn't handle non-finite values.
Results may differ from the reference program's by a relative error of at most 0.04.
Values may be sent and summed in bfloat16 or wider, within the bound.
A program may use at most 192 MiB of HBM per device.

```python
import math
import jax
import jax.numpy as jnp
from jax import lax

D = 4096
FF = 16384
DB = 1024
FB = 4096
VOL_TOK = 256
VOLS = 4
TOKENS = 1024
N_ROW = 4
N_COL = 4


def draw_up_weight(key, part):
    key_base = jax.random.fold_in(key, 11)
    key_noise = jax.random.fold_in(key_base, 1)
    key_common = jax.random.fold_in(key_base, 2)
    key_rough = jax.random.fold_in(key_base, 3)
    noise = jnp.clip(jax.random.normal(key_noise, (D, FF), jnp.float32), -6.0, 6.0)
    position = jnp.arange(D, dtype=jnp.float32) / (D - 1)
    rough = jax.random.uniform(key_rough, (D,), jnp.float32, 0.75, 1.25)
    rising = 0.5 + 1.5 * position
    common = jnp.clip(jax.random.normal(key_common, (FF,), jnp.float32), -4.0, 4.0)
    values = (noise + (rising * rough)[:, None] * common[None, :]) * D ** (-0.5)
    return values.astype(jnp.bfloat16)


def plant(drawn, key, smallest, top_value):
    longest = drawn.shape.index(max(drawn.shape))
    spots = []
    for shift in (0, 1):
        where = [jax.random.randint(jax.random.fold_in(key, axis), (), 0, length) for axis, length in enumerate(drawn.shape)]
        where[longest] = (where[longest] + shift) % drawn.shape[longest]
        spots.append(tuple(where))
    return drawn.at[spots[0]].set(smallest).at[spots[1]].set(top_value)


def shard_levels(stream_key, dims, split, smallest, largest):
    gain = 1.0
    for axis_at, parts in split:
        heights = jax.random.uniform(jax.random.fold_in(jax.random.fold_in(stream_key, 6), axis_at), (parts,), jnp.float32, smallest / len(split), largest / len(split))
        gain = gain * jnp.repeat(jnp.exp(heights), dims[axis_at] // parts).reshape((-1,) + (1,) * (len(dims) - 1 - axis_at))
    return gain


def scatter_about(rng, extent, spread, bound, shards=(), kind=jnp.bfloat16):
    result = spread * jax.random.normal(rng, extent, jnp.float32)
    if shards:
        result = result * shard_levels(rng, extent, shards, -0.22, 0.18)
    return jnp.clip(result, -bound, bound).astype(kind)


def setup_inputs(seed: int = 0) -> dict:
    keys = jax.random.split(jax.random.key(seed), 7)
    return {
        "tokens": scatter_about(keys[0], (TOKENS, D), 1.0, 6.0, ((0, 8), (1, 4))),
        "timesteps": plant(jax.random.randint(keys[1], (VOLS,), 0, 1000), jax.random.fold_in(keys[1], 1), 0, 999).astype(jnp.int32),
        "ada_weight": scatter_about(keys[2], (3, D, D), D ** -0.5, 0.09375, ((1, 4), (2, 4))),
        "up_weight": draw_up_weight(jax.random.fold_in(keys[6], 71), 0),
        "down_weight": scatter_about(keys[4], (FF, D), FF ** -0.5, 0.046875, ((0, 4), (1, 4))),
        "cotangent": scatter_about(keys[5], (TOKENS, D), 1.0, 6.0, ((0, 8), (1, 4))),
    }


tanh_scale = math.sqrt(2.0 / math.pi)

def gelu_tanh(h):
    return 0.5 * h * (1.0 + jnp.tanh(tanh_scale * (h + 0.044715 * h * h * h)))

def gelu_slope(h):
    inner = jnp.tanh(tanh_scale * (h + 0.044715 * h * h * h))
    return 0.5 * (1.0 + inner) + 0.5 * h * (1.0 - inner * inner) * tanh_scale * (1.0 + 3.0 * 0.044715 * h * h)

def time_features(timesteps, width):
    half = width // 2
    freqs = jnp.exp(-math.log(10000.0) * jnp.arange(half, dtype=jnp.float32) / half)
    angles = timesteps.astype(jnp.float32)[:, None] * freqs[None, :]
    embed = jnp.concatenate([jnp.cos(angles), jnp.sin(angles)], axis=1)
    return jax.nn.silu(embed).astype(jnp.bfloat16)

def rounded(value):
    return lax.optimization_barrier(value.astype(jnp.bfloat16)).astype(jnp.float32)

def reference(tokens, timesteps, ada_weight, up_weight, down_weight, cotangent):
    cond = time_features(timesteps, D)
    mod = jnp.einsum('vi,kio->vko', cond.astype(jnp.float32), ada_weight.astype(jnp.float32), precision=lax.Precision.HIGHEST)
    per_token = jnp.repeat(mod, VOL_TOK, axis=0)
    shift = per_token[:, 0]
    scale = per_token[:, 1]
    gate = per_token[:, 2]
    x = tokens.astype(jnp.float32)
    mean = lax.optimization_barrier(jnp.sum(x, axis=1)) / D
    var = lax.optimization_barrier(jnp.sum(x * x, axis=1)) / D - mean * mean
    rstd = lax.rsqrt(var + 1e-06)
    normed = (x - mean[:, None]) * rstd[:, None]
    modulated = (normed * (1.0 + scale) + shift).astype(jnp.bfloat16)
    hidden = jnp.zeros((TOKENS, FF), jnp.float32)
    for blk in range(N_ROW):
        part = jnp.dot(modulated[:, blk * DB:(blk + 1) * DB], up_weight[blk * DB:(blk + 1) * DB], preferred_element_type=jnp.float32)
        hidden = hidden + rounded(part)
    act = gelu_tanh(hidden).astype(jnp.bfloat16)
    branch = jnp.zeros((TOKENS, D), jnp.float32)
    for blk in range(N_COL):
        part = jnp.dot(act[:, blk * FB:(blk + 1) * FB], down_weight[blk * FB:(blk + 1) * FB], preferred_element_type=jnp.float32)
        branch = branch + rounded(part)
    cot = cotangent.astype(jnp.float32)
    grad_branch = (cot * gate).astype(jnp.bfloat16)
    grad_down = lax.dot_general(act, grad_branch, (((0,), (0,)), ((), ())), preferred_element_type=jnp.float32)
    grad_act = jnp.zeros((TOKENS, FF), jnp.float32)
    for blk in range(N_ROW):
        part = lax.dot_general(grad_branch[:, blk * DB:(blk + 1) * DB], down_weight[:, blk * DB:(blk + 1) * DB], (((1,), (1,)), ((), ())), preferred_element_type=jnp.float32)
        grad_act = grad_act + rounded(part)
    grad_hidden = (grad_act * gelu_slope(hidden)).astype(jnp.bfloat16)
    grad_up = lax.dot_general(modulated, grad_hidden, (((0,), (0,)), ((), ())), preferred_element_type=jnp.float32)
    grad_mod_in = jnp.zeros((TOKENS, D), jnp.float32)
    for blk in range(N_COL):
        part = lax.dot_general(grad_hidden[:, blk * FB:(blk + 1) * FB], up_weight[:, blk * FB:(blk + 1) * FB], (((1,), (1,)), ((), ())), preferred_element_type=jnp.float32)
        grad_mod_in = grad_mod_in + rounded(part)
    grad_shift = lax.optimization_barrier(jnp.sum(grad_mod_in.reshape(VOLS, VOL_TOK, D), axis=1))
    grad_scale = lax.optimization_barrier(jnp.sum((grad_mod_in * normed).reshape(VOLS, VOL_TOK, D), axis=1))
    grad_gate = lax.optimization_barrier(jnp.sum((cot * branch).reshape(VOLS, VOL_TOK, D), axis=1))
    grad_mod = jnp.stack([grad_shift, grad_scale, grad_gate], axis=1)
    grad_ada = jnp.einsum('vi,vko->kio', cond.astype(jnp.float32), grad_mod, precision=lax.Precision.HIGHEST)
    grad_norm = grad_mod_in * (1.0 + scale)
    first = lax.optimization_barrier(jnp.sum(grad_norm, axis=1)) / D
    second = lax.optimization_barrier(jnp.sum(grad_norm * normed, axis=1)) / D
    grad_tokens = cot + rstd[:, None] * (grad_norm - first[:, None] - normed * second[:, None])
    return (grad_tokens.astype(jnp.bfloat16), grad_ada, grad_up, grad_down)
```

```python
import functools
import math

import jax
import jax.numpy as jnp
from jax import lax
from jax.experimental import pallas as pl
from jax.experimental.pallas import tpu as pltpu
from jax.sharding import PartitionSpec as P

MESH = pl.DeviceIdType.MESH
F32 = jnp.float32
BF16 = jnp.bfloat16
VMEM = pl.BlockSpec(memory_space=pltpu.VMEM)
MIB = 1 << 20
tanh_scale = math.sqrt(2.0 / math.pi)


def time_features(timesteps, width):
    half = width // 2
    freqs = jnp.exp(-math.log(10000.0) * jnp.arange(half, dtype=jnp.float32) / half)
    angles = timesteps.astype(jnp.float32)[:, None] * freqs[None, :]
    embed = jnp.concatenate([jnp.cos(angles), jnp.sin(angles)], axis=1)
    return jax.nn.silu(embed).astype(jnp.bfloat16)


def remote(src, dst, send, recv, device):
    return pltpu.make_async_remote_copy(
        src_ref=src, dst_ref=dst, send_sem=send, recv_sem=recv, device_id=device, device_id_type=MESH
    )


def greet(devices):
    barrier = pltpu.get_barrier_semaphore()
    for device in devices:
        pl.semaphore_signal(barrier, inc=1, device_id=device, device_id_type=MESH)
    pl.semaphore_wait(barrier, len(devices))


def others(axis, count):
    me = lax.axis_index(axis)
    return [lax.rem(me + step, count) for step in range(1, count)]


def token_columns(packed, square):
    square[...] = jnp.zeros_like(square)
    square[0:8, :] = packed
    turned = jnp.transpose(square[...])
    return turned[:, 0:1], turned[:, 4:5]


def token_stats(total, squares, full_width):
    mean = total / full_width
    var = squares / full_width - mean * mean
    return mean, lax.rsqrt(var + 1e-06)


def enter_kernel(
    rows, cols, full_width, tok, cot, terms, sums, full, mod_out, sums_out,
    got_terms, got_sums, square, send_terms, recv_terms, send_sums, recv_sums, send_full, recv_full,
):
    row, col = lax.axis_index("row"), lax.axis_index("col")
    row_peers, col_peers = others("row", rows), others("col", cols)
    greet([{"row": p} for p in row_peers] + [{"col": p} for p in col_peers])
    for at, p in enumerate(row_peers):
        remote(sums, got_sums.at[row], send_sums.at[at], recv_sums.at[row], {"row": p}).start()
    for at, p in enumerate(col_peers):
        remote(terms.at[p], got_terms.at[col], send_terms.at[at], recv_terms.at[col], {"col": p}).start()
    mod = terms[col]
    for at, p in enumerate(col_peers):
        remote(terms.at[p], got_terms.at[p], send_terms.at[at], recv_terms.at[p], {"col": p}).wait_recv()
        mod = mod + got_terms[p]
    packed = sums[...]
    for at, p in enumerate(row_peers):
        remote(sums, got_sums.at[p], send_sums.at[at], recv_sums.at[p], {"row": p}).wait_recv()
        packed = packed + got_sums[p]
    mod_out[...] = mod
    sums_out[...] = packed
    mean, rstd = token_stats(*token_columns(packed, square), full_width)
    normed = (tok[...].astype(F32) - mean) * rstd
    full[0, col] = (normed * (1.0 + mod[1:2]) + mod[0:1]).astype(BF16)
    full[1, col] = (cot[...].astype(F32) * mod[2:3]).astype(BF16)
    for at, p in enumerate(col_peers):
        remote(full.at[:, col], full.at[:, col], send_full.at[at], recv_full.at[col], {"col": p}).start()
    for at, p in enumerate(col_peers):
        remote(full.at[:, p], full.at[:, p], send_full.at[at], recv_full.at[p], {"col": p}).wait_recv()
    for at, p in enumerate(row_peers):
        remote(sums, got_sums.at[row], send_sums.at[at], recv_sums.at[row], {"row": p}).wait_send()
    for at, p in enumerate(col_peers):
        remote(terms.at[p], got_terms.at[col], send_terms.at[at], recv_terms.at[col], {"col": p}).wait_send()
        remote(full.at[:, col], full.at[:, col], send_full.at[at], recv_full.at[col], {"col": p}).wait_send()


def enter(rows, cols, full_width, tok, cot, terms, sums):
    n, width = tok.shape
    dma = pltpu.SemaphoreType.DMA
    return pl.pallas_call(
        functools.partial(enter_kernel, rows, cols, full_width),
        out_shape=(
            jax.ShapeDtypeStruct((2, cols, n, width), BF16),
            jax.ShapeDtypeStruct((8, width), F32),
            jax.ShapeDtypeStruct((8, n), F32),
        ),
        in_specs=[VMEM] * 4,
        out_specs=(VMEM,) * 3,
        scratch_shapes=[
            pltpu.VMEM((cols, 8, width), F32),
            pltpu.VMEM((rows, 8, n), F32),
            pltpu.VMEM((128, n), F32),
            dma((cols,)), dma((cols,)), dma((rows,)), dma((rows,)), dma((cols,)), dma((cols,)),
        ],
        compiler_params=pltpu.CompilerParams(
            collective_id=0, has_side_effects=True, vmem_limit_bytes=24 * MIB
        ),
        name="enter",
    )(tok, cot, terms, sums)


def middle_kernel(
    n, chunks, hid, gact, act, ghid, got_h, got_g,
    rs_send_r, rs_send_l, rs_recv, ag_send_r, ag_send_l, ag_recv,
):
    r = lax.axis_index("row")
    from_right = n - 1 - r
    block = hid.shape[0] // n
    wide = hid.shape[1] // chunks
    ins, gots, outs = (hid, gact), (got_h, got_g), (act, ghid)
    right, left = {"row": lax.rem(r + 1, n)}, {"row": lax.rem(r + n - 1, n)}
    inner_right, inner_left = r < n - 1, r > 0

    barrier = pltpu.get_barrier_semaphore()

    @pl.when(inner_right)
    def _():
        pl.semaphore_signal(barrier, inc=1, device_id=right, device_id_type=MESH)

    @pl.when(inner_left)
    def _():
        pl.semaphore_signal(barrier, inc=1, device_id=left, device_id_type=MESH)

    @pl.when(inner_right & inner_left)
    def _():
        pl.semaphore_wait(barrier, 2)

    @pl.when(jnp.logical_not(inner_right & inner_left))
    def _():
        pl.semaphore_wait(barrier, 1)

    def columns(k):
        return pl.ds(pl.multiple_of(k * wide, wide), wide)

    def rows(j):
        return pl.ds(pl.multiple_of(j * block, block), block)

    def sum_right(w, k, j, own):
        src = ins[w].at[rows(j), columns(k)] if own else gots[w].at[j, :, columns(k)]
        return remote(src, gots[w].at[j, :, columns(k)], rs_send_r.at[w, k, j], rs_recv.at[w, k, j], right)

    def sum_left(w, k, j, own):
        slot = jnp.where(j == r - 1, n, j)
        src = ins[w].at[rows(j), columns(k)] if own else gots[w].at[j, :, columns(k)]
        return remote(src, gots[w].at[slot, :, columns(k)], rs_send_l.at[w, k, j], rs_recv.at[w, k, slot], left)

    def arrived(w, k, slot):
        remote(
            gots[w].at[slot, :, columns(k)], gots[w].at[slot, :, columns(k)],
            rs_send_r.at[w, k, 0], rs_recv.at[w, k, slot], right,
        ).wait_recv()

    def pass_right(w, k, j):
        at = outs[w].at[rows(j), columns(k)]
        return remote(at, at, ag_send_r.at[w, k, j], ag_recv.at[w, k, j], right)

    def pass_left(w, k, j):
        at = outs[w].at[rows(j), columns(k)]
        return remote(at, at, ag_send_l.at[w, k, j], ag_recv.at[w, k, j], left)

    def begin(k):
        @pl.when(r == 0)
        def _():
            for t in range(n - 1):
                for w in range(2):
                    sum_right(w, k, n - 1 - t, True).start()

        @pl.when(from_right == 0)
        def _():
            for t in range(n - 1):
                for w in range(2):
                    sum_left(w, k, t, True).start()

    def add(w, k, j):
        own = ins[w][rows(j), columns(k)].astype(F32)
        gots[w][j, :, columns(k)] = (gots[w][j, :, columns(k)].astype(F32) + own).astype(BF16)

    def sum_step(k, t):
        @pl.when((r > 0) & (r <= t))
        def _():
            j = n - 1 - t + r
            for w in range(2):
                arrived(w, k, j)
                add(w, k, j)
                sum_right(w, k, j, False).start()

        @pl.when((from_right > 0) & (from_right <= t))
        def _():
            j = t - from_right
            for w in range(2):
                arrived(w, k, j)
                add(w, k, j)
                sum_left(w, k, j, False).start()

    def finish(k):
        for w in range(2):
            @pl.when(inner_left)
            def _():
                arrived(w, k, r)

            @pl.when(inner_right)
            def _():
                arrived(w, k, n)

        def total(w):
            own = ins[w][rows(r), columns(k)].astype(F32)
            one = gots[w][r, :, columns(k)].astype(F32)
            two = gots[w][n, :, columns(k)].astype(F32)
            return own + jnp.where(inner_left, one, 0.0) + jnp.where(inner_right, two, 0.0)

        h = total(0)
        g = total(1)
        inner = jnp.tanh(tanh_scale * (h + 0.044715 * h * h * h))
        act[rows(r), columns(k)] = (0.5 * h * (1.0 + inner)).astype(BF16)
        slope = 0.5 * (1.0 + inner) + 0.5 * h * (1.0 - inner * inner) * tanh_scale * (
            1.0 + 3.0 * 0.044715 * h * h
        )
        ghid[rows(r), columns(k)] = (g * slope).astype(BF16)

    def pass_step(k, t):
        @pl.when(t <= r)
        def _():
            j = r - t
            for w in range(2):
                if t > 0:
                    pass_right(w, k, j).wait_recv()

                @pl.when(inner_right)
                def _():
                    pass_right(w, k, j).start()

        @pl.when(t <= from_right)
        def _():
            j = r + t
            for w in range(2):
                if t > 0:
                    pass_left(w, k, j).wait_recv()

                @pl.when(inner_left)
                def _():
                    pass_left(w, k, j).start()

    @pl.when(r == 0)
    def _():
        for w in range(2):
            gots[w][0] = jnp.zeros(gots[w].shape[1:], BF16)

    @pl.when(from_right == 0)
    def _():
        for w in range(2):
            gots[w][n] = jnp.zeros(gots[w].shape[1:], BF16)

    begin(0)

    def chunk(k, carry):
        @pl.when(k > 0)
        def _():
            pass_step(k - 1, 0)

        @pl.when(k + 1 < chunks)
        def _():
            begin(k + 1)

        for t in range(1, n):
            if t < n - 1:
                @pl.when(k < chunks)
                def _():
                    sum_step(k, t)

            @pl.when(k > 0)
            def _():
                pass_step(k - 1, t)

        @pl.when(k < chunks)
        def _():
            finish(k)

        return carry

    lax.fori_loop(0, chunks + 1, chunk, 0)

    def drain(k, carry):
        for j in range(n):
            for w in range(2):
                @pl.when(j > r)
                def _():
                    sum_right(w, k, j, False).wait_send()

                @pl.when(j < r)
                def _():
                    sum_left(w, k, j, False).wait_send()

                @pl.when((j <= r) & inner_right)
                def _():
                    pass_right(w, k, j).wait_send()

                @pl.when((j >= r) & inner_left)
                def _():
                    pass_left(w, k, j).wait_send()

        return carry

    lax.fori_loop(0, chunks, drain, 0)


def middle(rows, chunks, hid, gact):
    tokens, width = hid.shape
    block = tokens // rows
    dma = pltpu.SemaphoreType.DMA
    whole = jax.ShapeDtypeStruct((tokens, width), BF16)
    return pl.pallas_call(
        functools.partial(middle_kernel, rows, chunks),
        out_shape=(whole, whole),
        in_specs=[VMEM] * 2,
        out_specs=(VMEM,) * 2,
        scratch_shapes=[
            pltpu.VMEM((rows + 1, block, width), BF16),
            pltpu.VMEM((rows + 1, block, width), BF16),
            dma((2, chunks, rows)), dma((2, chunks, rows)), dma((2, chunks, rows + 1)),
            dma((2, chunks, rows)), dma((2, chunks, rows)), dma((2, chunks, rows)),
        ],
        compiler_params=pltpu.CompilerParams(
            collective_id=1, has_side_effects=True, vmem_limit_bytes=48 * MIB
        ),
        name="middle",
    )(hid, gact)


def leave_kernel(
    rows, cols, dps, full_width, branch, gmod, tok, cot, mod, sums, grad_tok, grad_mod,
    got, own_mod, got_mod, own_sums, got_sums, square,
    send_got, recv_got, send_mod, recv_mod, send_sums, recv_sums,
):
    row, col, dp = lax.axis_index("row"), lax.axis_index("col"), lax.axis_index("dp")
    row_peers, col_peers = others("row", rows), others("col", cols)
    group = cols * dps
    me = col * dps + dp
    mod_peers = [lax.rem(me + step, group) for step in range(1, group)]
    place = lambda p: {"col": p // dps, "dp": lax.rem(p, dps)}
    greet([{"row": p} for p in row_peers] + [place(p) for p in mod_peers])
    parts = (branch, gmod)
    for at, p in enumerate(col_peers):
        for w in range(2):
            remote(parts[w].at[p], got.at[w, col], send_got.at[w, at], recv_got.at[w, col], {"col": p}).start()
    mean, rstd = token_stats(*token_columns(sums[...], square), full_width)
    normed = (tok[...].astype(F32) - mean) * rstd
    cotf = cot[...].astype(F32)
    summed = []
    for w in range(2):
        total = parts[w][col].astype(F32)
        for at, p in enumerate(col_peers):
            remote(parts[w].at[p], got.at[w, p], send_got.at[w, at], recv_got.at[w, p], {"col": p}).wait_recv()
            total = total + got[w, p].astype(F32)
        summed.append(total)
    grad_norm = summed[1] * (1.0 + mod[1:2])
    lane = lax.broadcasted_iota(jnp.int32, square.shape, 1)
    one = jnp.sum(grad_norm, axis=1, keepdims=True)
    two = jnp.sum(grad_norm * normed, axis=1, keepdims=True)
    own_sums[...] = jnp.transpose(jnp.where(lane < 4, one, two))[0:8, :]
    for at, p in enumerate(row_peers):
        remote(own_sums, got_sums.at[row], send_sums.at[at], recv_sums.at[row], {"row": p}).start()
    own_mod[...] = jnp.zeros_like(own_mod)
    own_mod[0:1] = jnp.sum(summed[1], axis=0, keepdims=True)
    own_mod[1:2] = jnp.sum(summed[1] * normed, axis=0, keepdims=True)
    own_mod[2:3] = jnp.sum(cotf * summed[0], axis=0, keepdims=True)
    for at, p in enumerate(mod_peers):
        remote(own_mod, got_mod.at[me], send_mod.at[at], recv_mod.at[me], place(p)).start()
    packed = own_sums[...]
    for at, p in enumerate(row_peers):
        remote(own_sums, got_sums.at[p], send_sums.at[at], recv_sums.at[p], {"row": p}).wait_recv()
        packed = packed + got_sums[p]
    first, second = token_columns(packed, square)
    first = first / full_width
    second = second / full_width
    grad_tok[...] = (cotf + rstd * (grad_norm - first - normed * second)).astype(BF16)
    got_mod[me] = own_mod[...]
    for at, p in enumerate(mod_peers):
        remote(own_mod, got_mod.at[p], send_mod.at[at], recv_mod.at[p], place(p)).wait_recv()
    for v in range(cols):
        total = got_mod[v * dps]
        for d in range(1, dps):
            total = total + got_mod[v * dps + d]
        grad_mod[v] = total
    for at, p in enumerate(col_peers):
        for w in range(2):
            remote(parts[w].at[p], got.at[w, col], send_got.at[w, at], recv_got.at[w, col], {"col": p}).wait_send()
    for at, p in enumerate(row_peers):
        remote(own_sums, got_sums.at[row], send_sums.at[at], recv_sums.at[row], {"row": p}).wait_send()
    for at, p in enumerate(mod_peers):
        remote(own_mod, got_mod.at[me], send_mod.at[at], recv_mod.at[me], place(p)).wait_send()


def leave(rows, cols, dps, full_width, branch, gmod, tok, cot, mod, sums):
    n, width = tok.shape
    dma = pltpu.SemaphoreType.DMA
    group = cols * dps
    return pl.pallas_call(
        functools.partial(leave_kernel, rows, cols, dps, full_width),
        out_shape=(
            jax.ShapeDtypeStruct((n, width), BF16),
            jax.ShapeDtypeStruct((cols, 8, width), F32),
        ),
        in_specs=[VMEM] * 6,
        out_specs=(VMEM,) * 2,
        scratch_shapes=[
            pltpu.VMEM((2, cols, n, width), BF16),
            pltpu.VMEM((8, width), F32),
            pltpu.VMEM((group, 8, width), F32),
            pltpu.VMEM((8, n), F32),
            pltpu.VMEM((rows, 8, n), F32),
            pltpu.VMEM((128, n), F32),
            dma((2, cols)), dma((2, cols)), dma((group,)), dma((group,)), dma((rows,)), dma((rows,)),
        ],
        compiler_params=pltpu.CompilerParams(
            collective_id=2, has_side_effects=True, vmem_limit_bytes=24 * MIB
        ),
        name="leave",
    )(branch, gmod, tok, cot, mod, sums)


def body(tokens, timesteps, ada_weight, up_weight, down_weight, cotangent):
    rows = lax.axis_size("row")
    cols = lax.axis_size("col")
    dps = lax.axis_size("dp")
    n, width = tokens.shape
    full_width = width * rows
    in_width = ada_weight.shape[1]
    cond = time_features(timesteps, full_width)
    cond_part = lax.dynamic_slice_in_dim(cond, lax.axis_index("col") * in_width, in_width, 1)
    terms = jnp.einsum("vi,kio->vko", cond_part, ada_weight, preferred_element_type=F32)
    terms = jnp.pad(terms, ((0, 0), (0, 5), (0, 0)))
    x = tokens.astype(F32)
    total = jnp.sum(x, axis=1)
    squares = jnp.sum(x * x, axis=1)
    sums = jnp.stack([total] * 4 + [squares] * 4, axis=0)
    full, mod, sums = enter(rows, cols, full_width, tokens, cotangent, terms, sums)
    mod_full = full[0].reshape(cols * n, width)
    grad_full = full[1].reshape(cols * n, width)
    hid = jnp.dot(mod_full, up_weight, preferred_element_type=F32).astype(BF16)
    gact = lax.dot_general(
        grad_full, down_weight, (((1,), (1,)), ((), ())), preferred_element_type=F32
    ).astype(BF16)
    act, ghid = middle(rows, 8, hid, gact)
    branch = jnp.dot(act, down_weight, preferred_element_type=F32).astype(BF16)
    gmod = lax.dot_general(
        ghid, up_weight, (((1,), (1,)), ((), ())), preferred_element_type=F32
    ).astype(BF16)
    down_part = lax.dot_general(
        act, grad_full, (((0,), (0,)), ((), ())), preferred_element_type=F32
    )
    up_part = lax.dot_general(
        mod_full, ghid, (((0,), (0,)), ((), ())), preferred_element_type=F32
    )
    grad_up = lax.psum_scatter(
        up_part.astype(BF16), "dp", scatter_dimension=1, tiled=True
    ).astype(F32)
    grad_down = lax.psum_scatter(
        down_part.astype(BF16), "dp", scatter_dimension=0, tiled=True
    ).astype(F32)
    grad_tokens, grad_mod = leave(
        rows, cols, dps, full_width,
        branch.reshape(cols, n, width), gmod.reshape(cols, n, width), tokens, cotangent, mod, sums,
    )
    grad_ada = jnp.einsum(
        "vi,vko->kio", cond_part.astype(F32), grad_mod[:, :3], precision=lax.Precision.HIGHEST
    )
    return (grad_tokens, grad_ada, grad_up, grad_down)


def solution(mesh):
    return jax.shard_map(
        body,
        mesh=mesh,
        in_specs=(
            P(("col", "dp"), "row"),
            P(),
            P(None, "col", "row"),
            P("row", "col"),
            P("col", "row"),
            P(("col", "dp"), "row"),
        ),
        out_specs=(
            P(("col", "dp"), "row"),
            P(None, "col", "row"),
            P("row", ("col", "dp")),
            P(("col", "dp"), "row"),
        ),
        check_vma=False,
    )
```

```python
import functools
import math

import jax
import jax.numpy as jnp
from jax import lax
from jax.experimental import pallas as pl
from jax.experimental.pallas import tpu as pltpu
from jax.sharding import PartitionSpec as P

MESH = pl.DeviceIdType.MESH
F32 = jnp.float32
BF16 = jnp.bfloat16
VMEM = pl.BlockSpec(memory_space=pltpu.VMEM)
MIB = 1 << 20
tanh_scale = math.sqrt(2.0 / math.pi)


def time_features(timesteps, width):
    half = width // 2
    freqs = jnp.exp(-math.log(10000.0) * jnp.arange(half, dtype=jnp.float32) / half)
    angles = timesteps.astype(jnp.float32)[:, None] * freqs[None, :]
    embed = jnp.concatenate([jnp.cos(angles), jnp.sin(angles)], axis=1)
    return jax.nn.silu(embed).astype(jnp.bfloat16)


def remote(src, dst, send, recv, device):
    return pltpu.make_async_remote_copy(
        src_ref=src, dst_ref=dst, send_sem=send, recv_sem=recv, device_id=device, device_id_type=MESH
    )


def greet(devices):
    barrier = pltpu.get_barrier_semaphore()
    for device in devices:
        pl.semaphore_signal(barrier, inc=1, device_id=device, device_id_type=MESH)
    pl.semaphore_wait(barrier, len(devices))


def others(axis, count):
    me = lax.axis_index(axis)
    return [lax.rem(me + step, count) for step in range(1, count)]


def token_columns(packed, square):
    square[...] = jnp.zeros_like(square)
    square[0:8, :] = packed
    turned = jnp.transpose(square[...])
    return turned[:, 0:1], turned[:, 4:5]


def token_stats(total, squares, full_width):
    mean = total / full_width
    var = squares / full_width - mean * mean
    return mean, lax.rsqrt(var + 1e-06)


def enter_kernel(
    rows, cols, full_width, tok, cot, terms, sums, full, mod_out, sums_out,
    got_terms, got_sums, square, send_terms, recv_terms, send_sums, recv_sums, send_full, recv_full,
):
    row, col = lax.axis_index("row"), lax.axis_index("col")
    row_peers, col_peers = others("row", rows), others("col", cols)
    greet([{"row": p} for p in row_peers] + [{"col": p} for p in col_peers])
    for at, p in enumerate(row_peers):
        remote(sums, got_sums.at[row], send_sums.at[at], recv_sums.at[row], {"row": p}).start()
    for at, p in enumerate(col_peers):
        remote(terms.at[p], got_terms.at[col], send_terms.at[at], recv_terms.at[col], {"col": p}).start()
    mod = terms[col]
    for at, p in enumerate(col_peers):
        remote(terms.at[p], got_terms.at[p], send_terms.at[at], recv_terms.at[p], {"col": p}).wait_recv()
        mod = mod + got_terms[p]
    packed = sums[...]
    for at, p in enumerate(row_peers):
        remote(sums, got_sums.at[p], send_sums.at[at], recv_sums.at[p], {"row": p}).wait_recv()
        packed = packed + got_sums[p]
    mod_out[...] = mod
    sums_out[...] = packed
    mean, rstd = token_stats(*token_columns(packed, square), full_width)
    normed = (tok[...].astype(F32) - mean) * rstd
    full[0, col] = (normed * (1.0 + mod[1:2]) + mod[0:1]).astype(BF16)
    full[1, col] = (cot[...].astype(F32) * mod[2:3]).astype(BF16)
    for at, p in enumerate(col_peers):
        remote(full.at[:, col], full.at[:, col], send_full.at[at], recv_full.at[col], {"col": p}).start()
    for at, p in enumerate(col_peers):
        remote(full.at[:, p], full.at[:, p], send_full.at[at], recv_full.at[p], {"col": p}).wait_recv()
    for at, p in enumerate(row_peers):
        remote(sums, got_sums.at[row], send_sums.at[at], recv_sums.at[row], {"row": p}).wait_send()
    for at, p in enumerate(col_peers):
        remote(terms.at[p], got_terms.at[col], send_terms.at[at], recv_terms.at[col], {"col": p}).wait_send()
        remote(full.at[:, col], full.at[:, col], send_full.at[at], recv_full.at[col], {"col": p}).wait_send()


def enter(rows, cols, full_width, tok, cot, terms, sums):
    n, width = tok.shape
    dma = pltpu.SemaphoreType.DMA
    return pl.pallas_call(
        functools.partial(enter_kernel, rows, cols, full_width),
        out_shape=(
            jax.ShapeDtypeStruct((2, cols, n, width), BF16),
            jax.ShapeDtypeStruct((8, width), F32),
            jax.ShapeDtypeStruct((8, n), F32),
        ),
        in_specs=[VMEM] * 4,
        out_specs=(VMEM,) * 3,
        scratch_shapes=[
            pltpu.VMEM((cols, 8, width), F32),
            pltpu.VMEM((rows, 8, n), F32),
            pltpu.VMEM((128, n), F32),
            dma((cols,)), dma((cols,)), dma((rows,)), dma((rows,)), dma((cols,)), dma((cols,)),
        ],
        compiler_params=pltpu.CompilerParams(
            collective_id=0, has_side_effects=True, vmem_limit_bytes=24 * MIB
        ),
        name="enter",
    )(tok, cot, terms, sums)


def middle_kernel(
    n, chunks, mod_full, grad_full, up, down, act, ghid, hid, gact, up_in, down_in, got_h, got_g,
    load_up, load_down, rs_send_r, rs_send_l, rs_recv, ag_send_r, ag_send_l, ag_recv,
):
    r = lax.axis_index("row")
    from_right = n - 1 - r
    block = hid.shape[0] // n
    wide = hid.shape[1] // chunks
    ins, gots, outs = (hid, gact), (got_h, got_g), (act, ghid)
    right, left = {"row": lax.rem(r + 1, n)}, {"row": lax.rem(r + n - 1, n)}
    inner_right, inner_left = r < n - 1, r > 0

    for k in range(chunks):
        for load in (
            pltpu.make_async_copy(
                up.at[:, k * wide:(k + 1) * wide], up_in.at[:, k * wide:(k + 1) * wide], load_up.at[k]
            ),
            pltpu.make_async_copy(
                down.at[k * wide:(k + 1) * wide], down_in.at[k * wide:(k + 1) * wide], load_down.at[k]
            ),
        ):
            load.start()

    barrier = pltpu.get_barrier_semaphore()

    @pl.when(inner_right)
    def _():
        pl.semaphore_signal(barrier, inc=1, device_id=right, device_id_type=MESH)

    @pl.when(inner_left)
    def _():
        pl.semaphore_signal(barrier, inc=1, device_id=left, device_id_type=MESH)

    @pl.when(inner_right & inner_left)
    def _():
        pl.semaphore_wait(barrier, 2)

    @pl.when(jnp.logical_not(inner_right & inner_left))
    def _():
        pl.semaphore_wait(barrier, 1)

    def columns(k):
        return pl.ds(pl.multiple_of(k * wide, wide), wide)

    def rows(j):
        return pl.ds(pl.multiple_of(j * block, block), block)

    def loads(k):
        return (
            pltpu.make_async_copy(up.at[:, columns(k)], up_in.at[:, columns(k)], load_up.at[k]),
            pltpu.make_async_copy(down.at[columns(k)], down_in.at[columns(k)], load_down.at[k]),
        )

    def multiply(k):
        for load in loads(k):
            load.wait()
        hid[:, columns(k)] = jnp.dot(
            mod_full[...], up_in[:, columns(k)], preferred_element_type=F32
        ).astype(BF16)
        gact[:, columns(k)] = lax.dot_general(
            grad_full[...], down_in[columns(k)], (((1,), (1,)), ((), ())), preferred_element_type=F32
        ).astype(BF16)

    def sum_right(w, k, j, own):
        src = ins[w].at[rows(j), columns(k)] if own else gots[w].at[j, :, columns(k)]
        return remote(src, gots[w].at[j, :, columns(k)], rs_send_r.at[w, k, j], rs_recv.at[w, k, j], right)

    def sum_left(w, k, j, own):
        slot = jnp.where(j == r - 1, n, j)
        src = ins[w].at[rows(j), columns(k)] if own else gots[w].at[j, :, columns(k)]
        return remote(src, gots[w].at[slot, :, columns(k)], rs_send_l.at[w, k, j], rs_recv.at[w, k, slot], left)

    def arrived(w, k, slot):
        remote(
            gots[w].at[slot, :, columns(k)], gots[w].at[slot, :, columns(k)],
            rs_send_r.at[w, k, 0], rs_recv.at[w, k, slot], right,
        ).wait_recv()

    def pass_right(w, k, j):
        at = outs[w].at[rows(j), columns(k)]
        return remote(at, at, ag_send_r.at[w, k, j], ag_recv.at[w, k, j], right)

    def pass_left(w, k, j):
        at = outs[w].at[rows(j), columns(k)]
        return remote(at, at, ag_send_l.at[w, k, j], ag_recv.at[w, k, j], left)

    def begin(k):
        @pl.when(r == 0)
        def _():
            for t in range(n - 1):
                for w in range(2):
                    sum_right(w, k, n - 1 - t, True).start()

        @pl.when(from_right == 0)
        def _():
            for t in range(n - 1):
                for w in range(2):
                    sum_left(w, k, t, True).start()

    def add(w, k, j):
        own = ins[w][rows(j), columns(k)].astype(F32)
        gots[w][j, :, columns(k)] = (gots[w][j, :, columns(k)].astype(F32) + own).astype(BF16)

    def sum_step(k, t):
        @pl.when((r > 0) & (r <= t))
        def _():
            j = n - 1 - t + r
            for w in range(2):
                arrived(w, k, j)
                add(w, k, j)
                sum_right(w, k, j, False).start()

        @pl.when((from_right > 0) & (from_right <= t))
        def _():
            j = t - from_right
            for w in range(2):
                arrived(w, k, j)
                add(w, k, j)
                sum_left(w, k, j, False).start()

    def finish(k):
        for w in range(2):
            @pl.when(inner_left)
            def _():
                arrived(w, k, r)

            @pl.when(inner_right)
            def _():
                arrived(w, k, n)

        def total(w):
            own = ins[w][rows(r), columns(k)].astype(F32)
            one = gots[w][r, :, columns(k)].astype(F32)
            two = gots[w][n, :, columns(k)].astype(F32)
            return own + jnp.where(inner_left, one, 0.0) + jnp.where(inner_right, two, 0.0)

        h = total(0)
        g = total(1)
        inner = jnp.tanh(tanh_scale * (h + 0.044715 * h * h * h))
        act[rows(r), columns(k)] = (0.5 * h * (1.0 + inner)).astype(BF16)
        slope = 0.5 * (1.0 + inner) + 0.5 * h * (1.0 - inner * inner) * tanh_scale * (
            1.0 + 3.0 * 0.044715 * h * h
        )
        ghid[rows(r), columns(k)] = (g * slope).astype(BF16)

    def pass_step(k, t):
        @pl.when(t <= r)
        def _():
            j = r - t
            for w in range(2):
                if t > 0:
                    pass_right(w, k, j).wait_recv()

                @pl.when(inner_right)
                def _():
                    pass_right(w, k, j).start()

        @pl.when(t <= from_right)
        def _():
            j = r + t
            for w in range(2):
                if t > 0:
                    pass_left(w, k, j).wait_recv()

                @pl.when(inner_left)
                def _():
                    pass_left(w, k, j).start()

    @pl.when(r == 0)
    def _():
        for w in range(2):
            gots[w][0] = jnp.zeros(gots[w].shape[1:], BF16)

    @pl.when(from_right == 0)
    def _():
        for w in range(2):
            gots[w][n] = jnp.zeros(gots[w].shape[1:], BF16)

    multiply(0)
    begin(0)

    def chunk(k, carry):
        @pl.when(k > 0)
        def _():
            pass_step(k - 1, 0)

        @pl.when(k + 1 < chunks)
        def _():
            multiply(k + 1)
            begin(k + 1)

        for t in range(1, n):
            if t < n - 1:
                @pl.when(k < chunks)
                def _():
                    sum_step(k, t)

            @pl.when(k > 0)
            def _():
                pass_step(k - 1, t)

        @pl.when(k < chunks)
        def _():
            finish(k)

        return carry

    lax.fori_loop(0, chunks + 1, chunk, 0)

    def drain(k, carry):
        for j in range(n):
            for w in range(2):
                @pl.when(j > r)
                def _():
                    sum_right(w, k, j, False).wait_send()

                @pl.when(j < r)
                def _():
                    sum_left(w, k, j, False).wait_send()

                @pl.when((j <= r) & inner_right)
                def _():
                    pass_right(w, k, j).wait_send()

                @pl.when((j >= r) & inner_left)
                def _():
                    pass_left(w, k, j).wait_send()

        return carry

    lax.fori_loop(0, chunks, drain, 0)


def middle(rows, chunks, mod_full, grad_full, up, down):
    tokens, width = mod_full.shape[0], up.shape[1]
    block = tokens // rows
    dma = pltpu.SemaphoreType.DMA
    whole = jax.ShapeDtypeStruct((tokens, width), BF16)
    return pl.pallas_call(
        functools.partial(middle_kernel, rows, chunks),
        out_shape=(whole, whole),
        in_specs=[VMEM] * 2 + [pl.BlockSpec(memory_space=pl.ANY)] * 2,
        out_specs=(VMEM,) * 2,
        scratch_shapes=[
            pltpu.VMEM((tokens, width), BF16),
            pltpu.VMEM((tokens, width), BF16),
            pltpu.VMEM(up.shape, BF16),
            pltpu.VMEM(down.shape, BF16),
            pltpu.VMEM((rows + 1, block, width), BF16),
            pltpu.VMEM((rows + 1, block, width), BF16),
            dma((chunks,)), dma((chunks,)),
            dma((2, chunks, rows)), dma((2, chunks, rows)), dma((2, chunks, rows + 1)),
            dma((2, chunks, rows)), dma((2, chunks, rows)), dma((2, chunks, rows)),
        ],
        compiler_params=pltpu.CompilerParams(
            collective_id=1, has_side_effects=True, vmem_limit_bytes=56 * MIB
        ),
        name="middle",
    )(mod_full, grad_full, up, down)


def leave_kernel(
    rows, cols, dps, full_width, summed, tok, cot, mod, sums, grad_tok, grad_mod,
    own_mod, got_mod, own_sums, got_sums, square,
    send_mod, recv_mod, send_sums, recv_sums,
):
    row, col, dp = lax.axis_index("row"), lax.axis_index("col"), lax.axis_index("dp")
    row_peers = others("row", rows)
    group = cols * dps
    me = col * dps + dp
    mod_peers = [lax.rem(me + step, group) for step in range(1, group)]
    place = lambda p: {"col": p // dps, "dp": lax.rem(p, dps)}
    greet([{"row": p} for p in row_peers] + [place(p) for p in mod_peers])
    mean, rstd = token_stats(*token_columns(sums[...], square), full_width)
    normed = (tok[...].astype(F32) - mean) * rstd
    cotf = cot[...].astype(F32)
    grad_norm = summed[1] * (1.0 + mod[1:2])
    lane = lax.broadcasted_iota(jnp.int32, square.shape, 1)
    one = jnp.sum(grad_norm, axis=1, keepdims=True)
    two = jnp.sum(grad_norm * normed, axis=1, keepdims=True)
    own_sums[...] = jnp.transpose(jnp.where(lane < 4, one, two))[0:8, :]
    for at, p in enumerate(row_peers):
        remote(own_sums, got_sums.at[row], send_sums.at[at], recv_sums.at[row], {"row": p}).start()
    own_mod[...] = jnp.zeros_like(own_mod)
    own_mod[0:1] = jnp.sum(summed[1], axis=0, keepdims=True)
    own_mod[1:2] = jnp.sum(summed[1] * normed, axis=0, keepdims=True)
    own_mod[2:3] = jnp.sum(cotf * summed[0], axis=0, keepdims=True)
    for at, p in enumerate(mod_peers):
        remote(own_mod, got_mod.at[me], send_mod.at[at], recv_mod.at[me], place(p)).start()
    packed = own_sums[...]
    for at, p in enumerate(row_peers):
        remote(own_sums, got_sums.at[p], send_sums.at[at], recv_sums.at[p], {"row": p}).wait_recv()
        packed = packed + got_sums[p]
    first, second = token_columns(packed, square)
    first = first / full_width
    second = second / full_width
    grad_tok[...] = (cotf + rstd * (grad_norm - first - normed * second)).astype(BF16)
    got_mod[me] = own_mod[...]
    for at, p in enumerate(mod_peers):
        remote(own_mod, got_mod.at[p], send_mod.at[at], recv_mod.at[p], place(p)).wait_recv()
    for v in range(cols):
        total = got_mod[v * dps]
        for d in range(1, dps):
            total = total + got_mod[v * dps + d]
        grad_mod[v] = total
    for at, p in enumerate(row_peers):
        remote(own_sums, got_sums.at[row], send_sums.at[at], recv_sums.at[row], {"row": p}).wait_send()
    for at, p in enumerate(mod_peers):
        remote(own_mod, got_mod.at[me], send_mod.at[at], recv_mod.at[me], place(p)).wait_send()


def leave(rows, cols, dps, full_width, summed, tok, cot, mod, sums):
    n, width = tok.shape
    dma = pltpu.SemaphoreType.DMA
    group = cols * dps
    return pl.pallas_call(
        functools.partial(leave_kernel, rows, cols, dps, full_width),
        out_shape=(
            jax.ShapeDtypeStruct((n, width), BF16),
            jax.ShapeDtypeStruct((cols, 8, width), F32),
        ),
        in_specs=[VMEM] * 5,
        out_specs=(VMEM,) * 2,
        scratch_shapes=[
            pltpu.VMEM((8, width), F32),
            pltpu.VMEM((group, 8, width), F32),
            pltpu.VMEM((8, n), F32),
            pltpu.VMEM((rows, 8, n), F32),
            pltpu.VMEM((128, n), F32),
            dma((group,)), dma((group,)), dma((rows,)), dma((rows,)),
        ],
        compiler_params=pltpu.CompilerParams(
            collective_id=2, has_side_effects=True, vmem_limit_bytes=24 * MIB
        ),
        name="leave",
    )(summed, tok, cot, mod, sums)


def body(tokens, timesteps, ada_weight, up_weight, down_weight, cotangent):
    rows = lax.axis_size("row")
    cols = lax.axis_size("col")
    dps = lax.axis_size("dp")
    n, width = tokens.shape
    full_width = width * rows
    in_width = ada_weight.shape[1]
    cond = time_features(timesteps, full_width)
    cond_part = lax.dynamic_slice_in_dim(cond, lax.axis_index("col") * in_width, in_width, 1)
    terms = jnp.einsum("vi,kio->vko", cond_part, ada_weight, preferred_element_type=F32)
    terms = jnp.pad(terms, ((0, 0), (0, 5), (0, 0)))
    x = tokens.astype(F32)
    total = jnp.sum(x, axis=1)
    squares = jnp.sum(x * x, axis=1)
    sums = jnp.stack([total] * 4 + [squares] * 4, axis=0)
    full, mod, sums = enter(rows, cols, full_width, tokens, cotangent, terms, sums)
    mod_full = full[0].reshape(cols * n, width)
    grad_full = full[1].reshape(cols * n, width)
    act, ghid = middle(rows, 8, mod_full, grad_full, up_weight, down_weight)
    branch = jnp.dot(act, down_weight, preferred_element_type=F32).astype(BF16)
    gmod = lax.dot_general(
        ghid, up_weight, (((1,), (1,)), ((), ())), preferred_element_type=F32
    ).astype(BF16)
    col, dp = lax.axis_index("col"), lax.axis_index("dp")

    def block_of(c):
        return jnp.stack([lax.dynamic_slice_in_dim(a, c * n, n, 0) for a in (branch, gmod)])

    blocks = [block_of((col + step) % cols) for step in range(cols)]
    act, ghid, blocks = lax.optimization_barrier((act, ghid, blocks))
    arrived = [blocks[0]]
    for step in range(1, cols):
        pairs = [(c, (c + step) % cols) for c in range(cols)]
        arrived.append(lax.ppermute(blocks[step], "col", pairs))

    half = act.shape[1] // dps

    def down_part(d):
        mine = lax.dynamic_slice_in_dim(act, d * half, half, 1)
        return lax.dot_general(mine, grad_full, (((0,), (0,)), ((), ())), preferred_element_type=F32)

    def up_part(d):
        mine = lax.dynamic_slice_in_dim(ghid, d * half, half, 1)
        return lax.dot_general(mod_full, mine, (((0,), (0,)), ((), ())), preferred_element_type=F32)

    grads = []
    for part in (down_part, up_part):
        got = []
        for step in range(1, dps):
            pairs = [(d, (d + step) % dps) for d in range(dps)]
            got.append(lax.ppermute(part((dp + step) % dps).astype(BF16), "dp", pairs))
        total = part(dp)
        for g in got:
            total = total + g.astype(F32)
        grads.append(total)
    arrived, (grad_down, grad_up) = lax.optimization_barrier((arrived, grads))
    summed = arrived[0].astype(F32)
    for a in arrived[1:]:
        summed = summed + a.astype(F32)
    grad_tokens, grad_mod = leave(
        rows, cols, dps, full_width, summed, tokens, cotangent, mod, sums
    )
    condf = cond_part.astype(F32)
    grad_ada = condf[0][None, :, None] * grad_mod[0, :3][:, None, :]
    for v in range(1, cols):
        grad_ada = grad_ada + condf[v][None, :, None] * grad_mod[v, :3][:, None, :]
    return (grad_tokens, grad_ada, grad_up, grad_down)


def solution(mesh):
    return jax.shard_map(
        body,
        mesh=mesh,
        in_specs=(
            P(("col", "dp"), "row"),
            P(),
            P(None, "col", "row"),
            P("row", "col"),
            P("col", "row"),
            P(("col", "dp"), "row"),
        ),
        out_specs=(
            P(("col", "dp"), "row"),
            P(None, "col", "row"),
            P("row", ("col", "dp")),
            P(("col", "dp"), "row"),
        ),
        check_vma=False,
    )
```
